128 devices in a mesh: dp: 32 (over y, x, z_hi), expert: 4 (over z_lo, core).
Axes of the slice: x: 4, y: 4, z: 4 (z_hi: 2, z_lo: 2; z = z_hi * 2 + z_lo), core: 2. Of those that a mesh axis runs over, the one named last changes fastest.
Arguments:
- patches: bfloat16 [512, 256, 1152], P(('dp', 'expert')), may hold values from -6 to 6
- norm_gain: bfloat16 [1152], replicated, may hold values from 0.25 to 1.75
- router: bfloat16 [1152, 128], replicated, may hold values from -0.1875 to 0.1875
- expert_in: bfloat16 [128, 1152, 4304], P(('dp', 'expert')), may hold values from -0.1875 to 0.1875
- expert_out: bfloat16 [128, 4304, 1152], P(('dp', 'expert')), may hold values from -0.09375 to 0.09375
- post_gain: bfloat16 [1152], replicated, may hold values from 0.25 to 1.75
- key_query: bfloat16 [16, 1152], replicated, may hold values from -0.1875 to 0.1875
- value_proj: bfloat16 [1152, 1152], replicated, may hold values from -0.1875 to 0.1875
- out_proj: bfloat16 [1152, 1152], replicated, may hold values from -0.1875 to 0.1875
- text_embed: bfloat16 [512, 1152], P(('dp', 'expert')), may hold values from -6 to 6
- inverse_heat_exponent: float32 [1], replicated, may hold values from 1.8 to 2.6
- score_intercept: float32 [1], replicated, may hold values from -5 to -1.5
Outputs:
- pooled: float32 [512, 1152], P(('dp', 'expert'))
- pooled_grad: float32 [512, 1152], P(('dp', 'expert'))
- text_grad: float32 [512, 1152], P(('dp', 'expert'))
The draws below stay inside these ranges and needn't reach their ends.
All inputs are finite; a program needn't handle non-finite values.
Results may differ from the reference program's by a relative error of at most 0.015.
Values may be sent and summed in bfloat16 or wider, within the bound.
A program may use at most 128 MiB of HBM per device.

```python
import jax
import jax.numpy as jnp
from jax import lax

D = 1152
FF = 4304
HEADS = 16
HEAD_DIM = 72
PATCHES = 256
EXPERTS = 128
PAIRS = 512


def levels(stream_key, dims, pieces, smallest, top_value):
    level, own = 1.0, jax.random.fold_in(stream_key, 6)
    for position, blocks in pieces:
        heights = jnp.exp(jax.random.uniform(jax.random.fold_in(own, position), (blocks,), jnp.float32, smallest / len(pieces), top_value / len(pieces)))
        level = level * jnp.repeat(heights, dims[position] // blocks).reshape([-1 if axis == position else 1 for axis in range(len(dims))])
    return level


def centred(own_key, extent, scale, reach, cuts=(), held_as=jnp.bfloat16):
    array = scale * jax.random.normal(own_key, extent, jnp.float32)
    if cuts:
        array = array * levels(own_key, extent, cuts, -0.22, 0.18)
    return jnp.clip(array, -reach, reach).astype(held_as)


def setup_inputs(seed: int = 0) -> dict:
    splits = jax.random.split(jax.random.key(seed), 13)
    return {
        "patches": centred(splits[0], (PAIRS, PATCHES, D), 1.0, 6.0, ((0, 128),)),
        "norm_gain": jnp.clip(1.0 + 0.15 * jax.random.normal(splits[1], (D,), jnp.float32), 0.25, 1.75).astype(jnp.bfloat16),
        "router": centred(splits[2], (D, EXPERTS), D ** -0.5, 0.1875),
        "expert_in": centred(splits[3], (EXPERTS, D, FF), D ** -0.5, 0.1875, ((0, 128),)),
        "expert_out": centred(splits[4], (EXPERTS, FF, D), FF ** -0.5, 0.09375, ((0, 128),)),
        "post_gain": jnp.clip(1.0 + 0.15 * jax.random.normal(splits[5], (D,), jnp.float32), 0.25, 1.75).astype(jnp.bfloat16),
        "key_query": centred(splits[6], (HEADS, D), D ** -0.5, 0.1875),
        "value_proj": centred(splits[7], (D, HEADS * HEAD_DIM), D ** -0.5, 0.1875),
        "out_proj": centred(splits[8], (HEADS * HEAD_DIM, D), (HEADS * HEAD_DIM) ** -0.5, 0.1875),
        "text_embed": centred(splits[9], (PAIRS, D), 1.0, 6.0, ((0, 128),)),
        "inverse_heat_exponent": jnp.clip(jax.random.uniform(splits[10], (1,), jnp.float32, 1.8, 2.6), 1.8, 2.6),
        "score_intercept": jnp.clip(jax.random.uniform(splits[11], (1,), jnp.float32, -5.0, -1.5), -5.0, -1.5),
    }


def layer_norm(inputs_f32, gain_vector):
    center = lax.optimization_barrier(jnp.mean(inputs_f32, axis=-1, keepdims=True))
    shifted = inputs_f32 - center
    spread = lax.optimization_barrier(jnp.mean(shifted * shifted, axis=-1, keepdims=True))
    return shifted * lax.rsqrt(spread + 1e-06) * gain_vector.astype(jnp.float32)

def reference(patches, norm_gain, router, expert_in, expert_out, post_gain, key_query, value_proj, out_proj, text_embed, inverse_heat_exponent, score_intercept):

    def dispatch_one(one_image):
        normed = layer_norm(one_image.astype(jnp.float32), norm_gain).astype(jnp.bfloat16)
        logits = jnp.dot(normed, router, preferred_element_type=jnp.float32)
        slot_peak = lax.optimization_barrier(jnp.max(logits, axis=0, keepdims=True))
        weighted = jnp.exp(logits - slot_peak)
        dispatch = (weighted / lax.optimization_barrier(jnp.sum(weighted, axis=0, keepdims=True))).astype(jnp.bfloat16)
        slot_rows = jnp.dot(dispatch.T, normed, preferred_element_type=jnp.float32).astype(jnp.bfloat16)
        combine = jax.nn.softmax(logits, axis=1).astype(jnp.bfloat16)
        return (slot_rows, combine)
    slot_in, combine = lax.map(dispatch_one, patches)
    by_expert = jnp.swapaxes(slot_in, 0, 1)

    def expert_one(operands):
        expert_rows, first_weight, second_weight = operands
        hidden = jax.nn.gelu(jnp.dot(expert_rows, first_weight, preferred_element_type=jnp.float32), approximate=True).astype(jnp.bfloat16)
        return jnp.dot(hidden, second_weight, preferred_element_type=jnp.float32).astype(jnp.bfloat16)
    slot_out = jnp.swapaxes(lax.map(expert_one, (by_expert, expert_in, expert_out)), 0, 1)

    def pool_one(operands):
        one_image, weights, outputs = operands
        mixed_tokens = one_image.astype(jnp.float32) + jnp.dot(weights, outputs, preferred_element_type=jnp.float32)
        pool_in = layer_norm(mixed_tokens, post_gain).astype(jnp.bfloat16)
        scores = jnp.dot(pool_in, key_query.T, preferred_element_type=jnp.float32)
        head_peak = lax.optimization_barrier(jnp.max(scores, axis=0, keepdims=True))
        attend = jnp.exp(scores - head_peak)
        total_mass = lax.optimization_barrier(jnp.sum(attend, axis=0))
        summed = jnp.dot(attend.astype(jnp.bfloat16).T, pool_in, preferred_element_type=jnp.float32)
        return (summed / total_mass[:, None]).astype(jnp.bfloat16)
    headed = lax.map(pool_one, (patches, combine, slot_out))
    value_heads = value_proj.reshape(D, HEADS, HEAD_DIM).astype(jnp.float32)
    values = jnp.einsum('phd,dhe->phe', headed.astype(jnp.float32), value_heads).astype(jnp.bfloat16)
    pooled = jnp.dot(values.reshape(PAIRS, HEADS * HEAD_DIM), out_proj, preferred_element_type=jnp.float32)
    img_norm = jnp.sqrt(lax.optimization_barrier(jnp.sum(pooled * pooled, axis=1, keepdims=True)) + 1e-06)
    picture_direction_matrix = pooled / img_norm
    text_f32 = text_embed.astype(jnp.float32)
    txt_norm = jnp.sqrt(lax.optimization_barrier(jnp.sum(text_f32 * text_f32, axis=1, keepdims=True)) + 1e-06)
    caption_direction_matrix = text_f32 / txt_norm
    inverse_heat_multiplier = jnp.exp(inverse_heat_exponent[0])
    couple_score_matrix = inverse_heat_multiplier * jnp.dot(picture_direction_matrix, caption_direction_matrix.T, precision=lax.Precision.HIGHEST) + score_intercept[0]
    labels = 2.0 * jnp.eye(PAIRS, dtype=jnp.float32) - 1.0
    couple_coefficient = -labels * jax.nn.sigmoid(-labels * couple_score_matrix) / PAIRS
    picture_direction_derivative = inverse_heat_multiplier * jnp.dot(couple_coefficient, caption_direction_matrix, precision=lax.Precision.HIGHEST)
    caption_direction_derivative = inverse_heat_multiplier * jnp.dot(couple_coefficient.T, picture_direction_matrix, precision=lax.Precision.HIGHEST)
    pooled_grad = (picture_direction_derivative - picture_direction_matrix * lax.optimization_barrier(jnp.sum(picture_direction_matrix * picture_direction_derivative, axis=1, keepdims=True))) / img_norm
    text_grad = (caption_direction_derivative - caption_direction_matrix * lax.optimization_barrier(jnp.sum(caption_direction_matrix * caption_direction_derivative, axis=1, keepdims=True))) / txt_norm
    return (pooled, pooled_grad, text_grad)
```

```python
import functools

import jax
import jax.numpy as jnp
from jax import lax
from jax.experimental import pallas as pl
from jax.experimental.pallas import tpu as pltpu
from jax.sharding import PartitionSpec as P

MESH = pl.DeviceIdType.MESH
BF16, F32 = jnp.bfloat16, jnp.float32
BY_ROWS = (((1,), (1,)), ((), ()))
BY_COLUMNS = (((0,), (0,)), ((), ()))
EPS = 1e-6
GROUP = 2
STRIDE = 37
HIDDEN_STEP = 512
OUT_STEP = 384


def dot(a, b, dims=None):
    if dims is None:
        return jnp.dot(a, b, preferred_element_type=F32)
    return lax.dot_general(a, b, dims, preferred_element_type=F32)


def layer_norm(inputs, gain):
    center = jnp.mean(inputs, axis=1, keepdims=True)
    shifted = inputs - center
    spread = jnp.mean(shifted * shifted, axis=1, keepdims=True)
    return shifted * lax.rsqrt(spread + EPS) * gain


def norm_of(rows):
    return jnp.sqrt(jnp.sum(rows * rows, axis=1, keepdims=True) + EPS)


def split_dot(rows, table, dims=None):
    high = rows.astype(BF16)
    low = (rows - high.astype(F32)).astype(BF16)
    both = dot(jnp.concatenate([high.astype(F32), low.astype(F32)], axis=0).astype(BF16), table, dims)
    return both[: rows.shape[0]] + both[rows.shape[0] :]


def iota(shape, axis):
    return lax.broadcasted_iota(jnp.int32, shape, axis)


def kernel(
    patches_hbm, norm_gain_ref, router_ref, in_hbm, out_hbm, post_gain_ref, query_ref, value_hbm, proj_hbm,
    text_ref, heat_ref, intercept_ref,
    pooled_ref, pooled_grad_ref, text_grad_ref,
    patches, w_in, w_out, w_value, w_proj,
    sent, rows, answers, returned, expert_x, hidden, expert_y, normed_buf, dispatch_buf, combine_buf, headed,
    texts, text_pair, units, unit_pair, parts_out, parts_in,
    patch_sem, weight_sem, send_sem, recv_sem, near_send, near_recv,
):
    expert_size = lax.axis_size("expert")
    count = lax.axis_size("dp") * expert_size
    chips = count // 2
    me = lax.axis_index("dp") * expert_size + lax.axis_index("expert")
    core = lax.rem(me, 2)
    chip = me // 2
    sibling = me + 1 - 2 * core
    images, patch_count, width = patches.shape
    slots = router_ref.shape[1]
    heads = query_ref.shape[0]
    groups = images // GROUP

    def place(target):
        return (target // expert_size, lax.rem(target, expert_size))

    patch_copies = [
        pltpu.make_async_copy(patches_hbm.at[i], patches.at[i], patch_sem.at[i]) for i in range(images)
    ]
    weight_copies = [
        pltpu.make_async_copy(source, target, weight_sem.at[n])
        for n, (source, target) in enumerate(
            [(in_hbm.at[0], w_in), (out_hbm.at[0], w_out), (value_hbm, w_value), (proj_hbm, w_proj)]
        )
    ]
    for copy in patch_copies + weight_copies:
        copy.start()

    barrier = pltpu.get_barrier_semaphore()

    @pl.loop(1, count)
    def _(k):
        pl.semaphore_signal(barrier, inc=1, device_id=place(lax.rem(me + k, count)), device_id_type=MESH)

    def to_all(source, target, n):
        @pl.loop(1, count)
        def _(k):
            to = lax.rem(me + k * STRIDE, count)
            pltpu.make_async_remote_copy(
                src_ref=source.at[to], dst_ref=target.at[me], send_sem=send_sem.at[n], recv_sem=recv_sem.at[n],
                device_id=place(to), device_id_type=MESH,
            ).start()

        pltpu.make_async_copy(source.at[me], target.at[me], recv_sem.at[n]).start()

    def from_all(target, n):
        pltpu.make_async_copy(target, target, recv_sem.at[n]).wait()

    def to_class(table, n):
        @pl.loop(1, chips)
        def _(k):
            to = lax.rem(chip + k * STRIDE, chips) * 2 + core
            pltpu.make_async_remote_copy(
                src_ref=table.at[chip], dst_ref=table.at[chip], send_sem=send_sem.at[n], recv_sem=recv_sem.at[n],
                device_id=place(to), device_id_type=MESH,
            ).start()

    def from_class(table, n):
        part = table.at[pl.ds(0, chips - 1)]
        pltpu.make_async_copy(part, part, recv_sem.at[n]).wait()

    def near_copy(source, target, n):
        return pltpu.make_async_remote_copy(
            src_ref=source, dst_ref=target, send_sem=near_send.at[n], recv_sem=near_recv.at[n],
            device_id=place(sibling), device_id_type=MESH,
        )

    norm_gain = norm_gain_ref[...].astype(F32)
    post_gain = post_gain_ref[...].astype(F32)

    def dispatch(group):
        for i in range(GROUP):
            image = group * GROUP + i
            patch_copies[image].wait()
            block = pl.ds(i * patch_count, patch_count)
            normed = layer_norm(patches[image].astype(F32), norm_gain).astype(BF16)
            normed_buf[block, :] = normed
            logits = dot(normed, router_ref[...])
            spread = (iota((slots, GROUP * slots), 1) == GROUP * iota((slots, GROUP * slots), 0) + i)
            spread = spread.astype(F32).astype(BF16)
            weighted = jnp.exp(logits - jnp.max(logits, axis=0, keepdims=True))
            weighted = (weighted / jnp.sum(weighted, axis=0, keepdims=True)).astype(BF16)
            dispatch_buf[block, :] = dot(weighted, spread).astype(BF16)
            mixing = jnp.exp(logits - jnp.max(logits, axis=1, keepdims=True))
            mixing = (mixing / jnp.sum(mixing, axis=1, keepdims=True)).astype(BF16)
            combine_buf[group, block, :] = dot(mixing, spread).astype(BF16)
        slot_in = dot(dispatch_buf[...], normed_buf[...], BY_COLUMNS).astype(BF16)
        sent[group] = slot_in.reshape(slots, GROUP, width)

    def experts(group):
        expert_x[...] = rows[group].reshape(count * GROUP, width)
        inner = w_in.shape[0]
        steps = inner // HIDDEN_STEP

        def hidden_step(first, size):
            pre = dot(expert_x[...], w_in[pl.ds(first, size), :], BY_ROWS)
            hidden[:, pl.ds(first, size)] = jax.nn.gelu(pre, approximate=True).astype(BF16)

        @pl.loop(0, steps)
        def _(k):
            hidden_step(pl.multiple_of(k * HIDDEN_STEP, HIDDEN_STEP), HIDDEN_STEP)

        hidden_step(steps * HIDDEN_STEP, inner - steps * HIDDEN_STEP)

        @pl.loop(0, width // OUT_STEP)
        def _(n):
            columns = pl.ds(pl.multiple_of(n * OUT_STEP, OUT_STEP), OUT_STEP)
            expert_y[:, columns] = dot(hidden[:, 0:inner], w_out[:, columns]).astype(BF16)

        answers[group] = expert_y[...].reshape(count, GROUP, width)

    def pool(group):
        slot_out = returned[group].reshape(slots * GROUP, width)
        for i in range(GROUP):
            image = group * GROUP + i
            block = pl.ds(i * patch_count, patch_count)
            mixed = patches[image].astype(F32) + dot(combine_buf[group, block, :], slot_out)
            pool_in = layer_norm(mixed, post_gain).astype(BF16)
            scores = dot(query_ref[...], pool_in, BY_ROWS)
            attend = jnp.exp(scores - jnp.max(scores, axis=1, keepdims=True))
            mass = jnp.sum(attend, axis=1, keepdims=True)
            headed[pl.ds(image * heads, heads), :] = (dot(attend.astype(BF16), pool_in) / mass).astype(BF16)

    dispatch(0)
    pl.semaphore_wait(barrier, count - 1)
    to_all(sent.at[0], rows.at[0], 0)
    dispatch(1)
    to_all(sent.at[1], rows.at[1], 1)
    weight_copies[0].wait()
    weight_copies[1].wait()
    from_all(rows.at[0], 0)
    experts(0)
    to_all(answers.at[0], returned.at[0], 2)
    from_all(rows.at[1], 1)
    experts(1)
    to_all(answers.at[1], returned.at[1], 3)

    text = text_ref[...]
    texts[chip] = text
    text_pair[0] = text
    to_class(texts, 4)
    near_text = near_copy(text_pair.at[0], text_pair.at[1], 0)
    near_text.start()

    from_all(returned.at[0], 2)
    pool(0)
    weight_copies[2].wait()
    weight_copies[3].wait()
    from_all(returned.at[1], 3)
    pool(1)

    full = dot(headed[...], w_value[...])
    head_width = width // heads
    head = lax.rem(iota(full.shape, 0), heads)
    column = iota(full.shape, 1)
    own_head = (column >= head * head_width) & (column < (head + 1) * head_width)
    values = jnp.sum(jnp.where(own_head, full, 0.0).reshape(images, heads, width), axis=1)
    pooled = dot(values.astype(BF16), w_proj[...])
    pooled_ref[...] = pooled
    img_norm = norm_of(pooled)
    unit = pooled / img_norm
    unit_pair[0] = unit
    near_unit = near_copy(unit_pair.at[0], unit_pair.at[1], 1)
    near_unit.start()
    units[chip] = unit.astype(BF16)
    to_class(units, 5)

    heat = jnp.exp(heat_ref[...])
    intercept = intercept_ref[...]
    pairs = images * count
    side = images * chips
    row, col = iota((2 * images, side), 0), iota((2 * images, side), 1)
    label = jnp.where((row < images) & (col == chip * images + row), 1.0, -1.0)

    def coefficients(cosines):
        scores = heat * cosines + intercept
        return -label * jax.nn.sigmoid(-label * scores) / pairs

    near_text.wait_recv()
    from_class(texts, 4)
    table = texts[...].reshape(side, width)
    table_norm = norm_of(table.astype(F32))
    table_norm = jnp.transpose(jnp.broadcast_to(table_norm, (side, 128)))[0:1, :]
    near_unit.wait_recv()
    cosines = split_dot(unit_pair[...].reshape(2 * images, width), table, BY_ROWS) / table_norm
    part = heat * split_dot(coefficients(cosines) / table_norm, table)
    parts_out[0] = part[images:]
    near_image = near_copy(parts_out.at[0], parts_in.at[0], 2)
    near_image.start()
    image_part = part[:images]

    chip_texts = text_pair[...].reshape(2 * images, width).astype(F32)
    chip_norms = norm_of(chip_texts)
    own_norm = chip_norms[:images]
    own_unit = chip_texts[:images] / own_norm
    near_image.wait_recv()
    grad = image_part + parts_in[0]
    pooled_grad_ref[...] = (grad - unit * jnp.sum(unit * grad, axis=1, keepdims=True)) / img_norm

    from_class(units, 5)
    table = units[...].reshape(side, width)
    cosines = dot(chip_texts.astype(BF16), table, BY_ROWS) / chip_norms
    part = heat * split_dot(coefficients(cosines), table)
    parts_out[1] = part[images:]
    near_words = near_copy(parts_out.at[1], parts_in.at[1], 3)
    near_words.start()
    near_words.wait_recv()
    grad = part[:images] + parts_in[1]
    text_grad_ref[...] = (grad - own_unit * jnp.sum(own_unit * grad, axis=1, keepdims=True)) / own_norm

    for n, buffer in enumerate([sent.at[0], sent.at[1], answers.at[0], answers.at[1]]):
        part_ref = buffer.at[pl.ds(0, count - 1)]
        pltpu.make_async_copy(part_ref, part_ref, send_sem.at[n]).wait()
    for n, buffer in [(4, texts), (5, units)]:
        part_ref = buffer.at[pl.ds(0, chips - 1)]
        pltpu.make_async_copy(part_ref, part_ref, send_sem.at[n]).wait()
    for copy in (near_text, near_unit, near_image, near_words):
        copy.wait_send()


def body(
    patches, norm_gain, router, expert_in, expert_out, post_gain, key_query, value_proj, out_proj, text_embed,
    inverse_heat_exponent, score_intercept,
):
    images, patch_count, width = patches.shape
    inner = expert_out.shape[1]
    slots, heads = router.shape[1], key_query.shape[0]
    count = lax.axis_size("dp") * lax.axis_size("expert")
    chips = count // 2
    groups = images // GROUP
    vmem = pl.BlockSpec(memory_space=pltpu.VMEM)
    hbm = pl.BlockSpec(memory_space=pl.ANY)
    inner_padded = -(-inner // 128) * 128
    traffic = (groups, count, GROUP, width)
    out = jax.ShapeDtypeStruct((images, width), F32)
    return pl.pallas_call(
        kernel,
        out_shape=(out, out, out),
        in_specs=[hbm, vmem, vmem, hbm, hbm, vmem, vmem, hbm, hbm, vmem, vmem, vmem],
        out_specs=(vmem, vmem, vmem),
        scratch_shapes=[
            pltpu.VMEM(patches.shape, BF16),
            pltpu.VMEM((inner, width), BF16),
            pltpu.VMEM((inner, width), BF16),
            pltpu.VMEM(value_proj.shape, BF16),
            pltpu.VMEM(out_proj.shape, BF16),
            pltpu.VMEM(traffic, BF16),
            pltpu.VMEM(traffic, BF16),
            pltpu.VMEM(traffic, BF16),
            pltpu.VMEM(traffic, BF16),
            pltpu.VMEM((count * GROUP, width), BF16),
            pltpu.VMEM((count * GROUP, inner_padded), BF16),
            pltpu.VMEM((count * GROUP, width), BF16),
            pltpu.VMEM((GROUP * patch_count, width), BF16),
            pltpu.VMEM((GROUP * patch_count, GROUP * slots), BF16),
            pltpu.VMEM((groups, GROUP * patch_count, GROUP * slots), BF16),
            pltpu.VMEM((images * heads, width), BF16),
            pltpu.VMEM((chips, images, width), BF16),
            pltpu.VMEM((2, images, width), BF16),
            pltpu.VMEM((chips, images, width), BF16),
            pltpu.VMEM((2, images, width), F32),
            pltpu.VMEM((2, images, width), F32),
            pltpu.VMEM((2, images, width), F32),
            pltpu.SemaphoreType.DMA((images,)),
            pltpu.SemaphoreType.DMA((4,)),
            pltpu.SemaphoreType.DMA((6,)),
            pltpu.SemaphoreType.DMA((6,)),
            pltpu.SemaphoreType.DMA((4,)),
            pltpu.SemaphoreType.DMA((4,)),
        ],
        compiler_params=pltpu.CompilerParams(
            collective_id=0, has_side_effects=True, vmem_limit_bytes=60 * 1024 * 1024
        ),
        cost_estimate=pl.CostEstimate(flops=12_000_000_000, bytes_accessed=40_000_000, transcendentals=4_000_000),
    )(
        patches, norm_gain.reshape(1, width), router, jnp.swapaxes(expert_in, 1, 2), expert_out,
        post_gain.reshape(1, width), key_query, value_proj, out_proj, text_embed,
        inverse_heat_exponent.reshape(1, 1), score_intercept.reshape(1, 1),
    )


def solution(mesh):
    split = ("dp", "expert")
    placed = (
        P(split, None, None), P(), P(), P(split, None, None), P(split, None, None), P(), P(), P(), P(),
        P(split, None), P(), P(),
    )
    return jax.shard_map(
        body, mesh=mesh, in_specs=placed,
        out_specs=(P(split, None), P(split, None), P(split, None)), check_vma=False,
    )
```

```python
import functools

import jax
import jax.numpy as jnp
from jax import lax
from jax.experimental import pallas as pl
from jax.experimental.pallas import tpu as pltpu
from jax.sharding import PartitionSpec as P

MESH = pl.DeviceIdType.MESH
BF16, F32 = jnp.bfloat16, jnp.float32
BY_ROWS = (((1,), (1,)), ((), ()))
BY_COLUMNS = (((0,), (0,)), ((), ()))
EPS = 1e-6
GROUP = 2
STRIDE = 37
RING = 8
HIDDEN_STEP = 2176
VMEM_BYTES = 60 * 1024 * 1024


def dot(a, b, dims=None):
    if dims is None:
        return jnp.dot(a, b, preferred_element_type=F32)
    return lax.dot_general(a, b, dims, preferred_element_type=F32)


def layer_norm(inputs, gain):
    center = jnp.mean(inputs, axis=1, keepdims=True)
    shifted = inputs - center
    spread = jnp.mean(shifted * shifted, axis=1, keepdims=True)
    return shifted * lax.rsqrt(spread + EPS) * gain


def norm_of(rows):
    return jnp.sqrt(jnp.sum(rows * rows, axis=1, keepdims=True) + EPS)


def split_dot(rows, table, dims=None):
    high = rows.astype(BF16)
    low = (rows - high.astype(F32)).astype(BF16)
    both = dot(jnp.concatenate([high.astype(F32), low.astype(F32)], axis=0).astype(BF16), table, dims)
    return both[: rows.shape[0]] + both[rows.shape[0] :]


def iota(shape, axis):
    return lax.broadcasted_iota(jnp.int32, shape, axis)


def kernel(
    patches_hbm, norm_gain_hbm, router_hbm, in_hbm, out_hbm, post_gain_hbm, query_hbm, value_hbm, proj_hbm,
    text_hbm, heat_ref, intercept_ref,
    result_ref,
    norm_gain_ref, router_ref, post_gain_ref, query_ref, text_ref,
    patches, w_in, w_out, w_value, w_proj,
    sent, rows, answers, returned, expert_x, hidden, normed_buf, dispatch_buf, combine_buf, headed,
    line_texts, texts, line_units, units, image_parts, image_sums, text_parts, text_sums,
    patch_sem, weight_sem, small_sem, send_sem, recv_sem,
):
    expert_size = lax.axis_size("expert")
    count = lax.axis_size("dp") * expert_size
    lines = count // RING
    me = lax.axis_index("dp") * expert_size + lax.axis_index("expert")
    line, spot = me // RING, lax.rem(me, RING)
    images, patch_count, width = patches.shape
    slots = router_ref.shape[1]
    heads = query_ref.shape[0]
    groups = images // GROUP

    def place(target):
        return (target // expert_size, lax.rem(target, expert_size))

    patch_copies = [
        pltpu.make_async_copy(patches_hbm.at[i], patches.at[i], patch_sem.at[i]) for i in range(images)
    ]
    inner_rows = pl.ds(0, in_hbm.shape[1])
    weight_copies = [
        pltpu.make_async_copy(source, target, weight_sem.at[n])
        for n, (source, target) in enumerate(
            [(in_hbm.at[0], w_in.at[inner_rows]), (out_hbm.at[0], w_out.at[inner_rows]), (value_hbm, w_value), (proj_hbm, w_proj)]
        )
    ]
    small_copies = [
        pltpu.make_async_copy(source, target, small_sem.at[n])
        for n, (source, target) in enumerate(
            [
                (norm_gain_hbm, norm_gain_ref), (router_hbm, router_ref), (post_gain_hbm, post_gain_ref),
                (query_hbm, query_ref), (text_hbm, text_ref),
            ]
        )
    ]
    for copy in patch_copies[:1] + small_copies + patch_copies[1:]:
        copy.start()
    for copy in weight_copies:
        copy.start(priority=1)

    barrier = pltpu.get_barrier_semaphore()

    @pl.loop(1, count)
    def _(k):
        pl.semaphore_signal(barrier, inc=1, device_id=place(lax.rem(me + k, count)), device_id_type=MESH)

    def to_all(source, target, n):
        @pl.loop(1, count)
        def _(k):
            to = lax.rem(me + k * STRIDE, count)
            pltpu.make_async_remote_copy(
                src_ref=source.at[to], dst_ref=target.at[me], send_sem=send_sem.at[n], recv_sem=recv_sem.at[n],
                device_id=place(to), device_id_type=MESH,
            ).start()

        pltpu.make_async_copy(source.at[me], target.at[me], recv_sem.at[n]).start()

    def have_left(buffer, n):
        part = buffer.at[pl.ds(0, buffer.shape[0] - 1)]
        pltpu.make_async_copy(part, part, send_sem.at[n]).wait()

    def from_all(target, n):
        pltpu.make_async_copy(target, target, recv_sem.at[n]).wait()

    def to_line(source, target, n):
        @pl.loop(1, RING)
        def _(k):
            to = lax.rem(spot + k, RING)
            pltpu.make_async_remote_copy(
                src_ref=source.at[to] if len(source.shape) == 3 else source, dst_ref=target.at[spot],
                send_sem=send_sem.at[n], recv_sem=recv_sem.at[n],
                device_id=place(line * RING + to), device_id_type=MESH,
            ).start()

    def to_lines(table, n):
        @pl.loop(1, lines)
        def _(k):
            to = lax.rem(line + k * 5, lines)
            pltpu.make_async_remote_copy(
                src_ref=table.at[line], dst_ref=table.at[line], send_sem=send_sem.at[n], recv_sem=recv_sem.at[n],
                device_id=place(to * RING + spot), device_id_type=MESH,
            ).start()

    def from_others(table, n):
        part = table.at[pl.ds(0, table.shape[0] - 1)]
        pltpu.make_async_copy(part, part, recv_sem.at[n]).wait()

    for copy in small_copies:
        copy.wait()
    norm_gain = norm_gain_ref[...].astype(F32).reshape(1, width)
    post_gain = post_gain_ref[...].astype(F32).reshape(1, width)

    def patch_wait(image):
        pltpu.make_async_copy(patches_hbm.at[image], patches.at[image], patch_sem.at[image]).wait()

    def spreading(i):
        shape = (slots, GROUP * slots)
        return (iota(shape, 1) == GROUP * iota(shape, 0) + i).astype(F32).astype(BF16)

    def block_of(i):
        return pl.ds(pl.multiple_of(i * patch_count, patch_count), patch_count)

    def dispatch(group):
        @pl.loop(0, GROUP)
        def _(i):
            image = group * GROUP + i
            block = block_of(i)
            patch_wait(image)
            normed = layer_norm(patches[image].astype(F32), norm_gain).astype(BF16)
            normed_buf[block, :] = normed
            logits = dot(normed, router_ref[...])
            spread = spreading(i)
            weighted = jnp.exp(logits - jnp.max(logits, axis=0, keepdims=True))
            weighted = (weighted / jnp.sum(weighted, axis=0, keepdims=True)).astype(BF16)
            dispatch_buf[block, :] = dot(weighted, spread).astype(BF16)
            mixing = jnp.exp(logits - jnp.max(logits, axis=1, keepdims=True))
            mixing = (mixing / jnp.sum(mixing, axis=1, keepdims=True)).astype(BF16)
            combine_buf[group, block, :] = dot(mixing, spread).astype(BF16)

        slot_in = dot(dispatch_buf[...], normed_buf[...], BY_COLUMNS).astype(BF16)
        sent[group] = slot_in.reshape(slots, GROUP, width)

    def experts(group):
        expert_x[...] = rows[group].reshape(count * GROUP, width)

        @pl.loop(0, hidden.shape[1] // HIDDEN_STEP)
        def _(k):
            part = pl.ds(pl.multiple_of(k * HIDDEN_STEP, HIDDEN_STEP), HIDDEN_STEP)
            pre = dot(expert_x[...], w_in[part, :], BY_ROWS)
            hidden[:, part] = jax.nn.gelu(pre, approximate=True).astype(BF16)

        answers[group] = dot(hidden[...], w_out[...]).astype(BF16).reshape(count, GROUP, width)

    def pool(group):
        @pl.loop(0, GROUP)
        def _(i):
            image = group * GROUP + i
            slot_out = returned[group].reshape(slots * GROUP, width)
            mixed = patches[image].astype(F32) + dot(combine_buf[group, block_of(i), :], slot_out)
            pool_in = layer_norm(mixed, post_gain).astype(BF16)
            scores = dot(query_ref[...], pool_in, BY_ROWS)
            attend = jnp.exp(scores - jnp.max(scores, axis=1, keepdims=True))
            mass = jnp.sum(attend, axis=1, keepdims=True)
            summed = dot(attend.astype(BF16), pool_in) / mass
            headed[pl.ds(pl.multiple_of(image * heads, heads), heads), :] = summed.astype(BF16)

    inner = in_hbm.shape[1]
    filler = w_in.shape[0] - inner
    w_in[pl.ds(inner, filler), :] = jnp.zeros((filler, width), BF16)
    w_out[pl.ds(inner, filler), :] = jnp.zeros((filler, width), BF16)

    @pl.loop(0, groups)
    def _(group):
        dispatch(group)

        @pl.when(group == 0)
        def _():
            pl.semaphore_wait(barrier, count - 1)

        @pl.when(group > 0)
        def _():
            have_left(sent.at[0], 0)

        to_all(sent.at[group], rows.at[group], group)

    weight_copies[0].wait()
    weight_copies[1].wait()

    @pl.loop(0, groups)
    def _(group):
        from_all(rows.at[group], group)
        experts(group)
        to_all(answers.at[group], returned.at[group], groups + group)

    text = text_ref[...]
    line_texts[spot] = text
    texts[line] = text
    to_line(line_texts.at[spot], line_texts, 4)
    to_lines(texts, 5)
    weight_copies[2].wait()
    weight_copies[3].wait()

    @pl.loop(0, groups)
    def _(group):
        from_all(returned.at[group], groups + group)
        pool(group)

    full = dot(headed[...], w_value[...])
    head_width = width // heads
    head = lax.rem(iota(full.shape, 0), heads)
    column = iota(full.shape, 1)
    own_head = (column >= head * head_width) & (column < (head + 1) * head_width)
    values = jnp.sum(jnp.where(own_head, full, 0.0).reshape(images, heads, width), axis=1)
    pooled = dot(values.astype(BF16), w_proj[...])
    result_ref[0] = pooled
    img_norm = norm_of(pooled)
    unit = pooled / img_norm
    line_units[spot] = unit.astype(BF16)
    units[line] = unit.astype(BF16)
    to_line(line_units.at[spot], line_units, 6)
    to_lines(units, 7)

    heat = jnp.exp(jnp.full((1, 1), heat_ref[0], F32))
    intercept = intercept_ref[0]
    pairs = images * count
    near, far = images * RING, images * lines
    row, col = iota((near, far), 0), iota((near, far), 1)
    own_row = (row >= spot * images) & (row < (spot + 1) * images)
    label = jnp.where(own_row & (row - spot * images == col - line * images), 1.0, -1.0)

    zeros = jnp.zeros((images, width), BF16)
    image_sums[spot] = zeros
    text_sums[spot] = zeros

    def own_block(part):
        return jnp.sum(jnp.where(own_row[:, 0:1], part, 0.0).reshape(RING, images, width), axis=0)

    def coefficients(cosines):
        scores = heat * cosines + intercept
        return -label * jax.nn.sigmoid(-label * scores) / pairs

    from_others(line_texts, 4)
    from_others(texts, 5)
    table = texts[...].reshape(far, width)
    table_norm = norm_of(table.astype(F32))
    table_norm = jnp.transpose(jnp.broadcast_to(table_norm, (far, 128)))[0:1, :]
    near_texts = line_texts[...].reshape(near, width)
    near_norms = norm_of(near_texts.astype(F32))
    text = text.astype(F32)
    text_norm = norm_of(text)
    unit_text = text / text_norm
    from_others(line_units, 6)
    cosines = dot(line_units[...].reshape(near, width), table, BY_ROWS) / table_norm
    part = heat * split_dot(coefficients(cosines) / table_norm, table)
    image_parts[...] = part.astype(BF16).reshape(RING, images, width)
    to_line(image_parts, image_sums, 8)
    own_image_part = own_block(part)

    from_others(units, 7)
    table = units[...].reshape(far, width)
    cosines = dot(near_texts, table, BY_ROWS) / near_norms
    part = heat * split_dot(coefficients(cosines), table)
    text_parts[...] = part.astype(BF16).reshape(RING, images, width)
    to_line(text_parts, text_sums, 9)
    own_text_part = own_block(part)

    from_others(image_sums, 8)
    grad = own_image_part + jnp.sum(image_sums[...].astype(F32), axis=0)
    result_ref[1] = (grad - unit * jnp.sum(unit * grad, axis=1, keepdims=True)) / img_norm
    from_others(text_sums, 9)
    grad = own_text_part + jnp.sum(text_sums[...].astype(F32), axis=0)
    result_ref[2] = (grad - unit_text * jnp.sum(unit_text * grad, axis=1, keepdims=True)) / text_norm

    blocks = [
        sent.at[1], answers.at[0], answers.at[1], line_texts, texts, line_units, units, image_parts, text_parts,
    ]
    for n, buffer in enumerate(blocks):
        have_left(buffer, n + 1)


def unstack(stacked_ref, pooled_ref, pooled_grad_ref, text_grad_ref, sem):
    copies = [
        pltpu.make_async_copy(stacked_ref.at[n], target, sem.at[n])
        for n, target in enumerate((pooled_ref, pooled_grad_ref, text_grad_ref))
    ]
    for copy in copies:
        copy.start()
    for copy in copies:
        copy.wait()


def body(
    patches, norm_gain, router, expert_in, expert_out, post_gain, key_query, value_proj, out_proj, text_embed,
    inverse_heat_exponent, score_intercept,
):
    images, patch_count, width = patches.shape
    inner = expert_out.shape[1]
    slots, heads = router.shape[1], key_query.shape[0]
    count = lax.axis_size("dp") * lax.axis_size("expert")
    groups = images // GROUP
    vmem = pl.BlockSpec(memory_space=pltpu.VMEM)
    hbm = pl.BlockSpec(memory_space=pl.ANY)
    filled = -(-inner // HIDDEN_STEP) * HIDDEN_STEP
    traffic = (groups, count, GROUP, width)
    out = jax.ShapeDtypeStruct((images, width), F32)
    result = pl.pallas_call(
        kernel,
        out_shape=jax.ShapeDtypeStruct((3, images, width), F32),
        in_specs=[hbm] * 10 + [pl.BlockSpec(memory_space=pltpu.SMEM)] * 2,
        out_specs=vmem,
        scratch_shapes=[
            pltpu.VMEM((width,), BF16),
            pltpu.VMEM(router.shape, BF16),
            pltpu.VMEM((width,), BF16),
            pltpu.VMEM(key_query.shape, BF16),
            pltpu.VMEM(text_embed.shape, BF16),
            pltpu.VMEM(patches.shape, BF16),
            pltpu.VMEM((filled, width), BF16),
            pltpu.VMEM((filled, width), BF16),
            pltpu.VMEM(value_proj.shape, BF16),
            pltpu.VMEM(out_proj.shape, BF16),
            pltpu.VMEM(traffic, BF16),
            pltpu.VMEM(traffic, BF16),
            pltpu.VMEM(traffic, BF16),
            pltpu.VMEM(traffic, BF16),
            pltpu.VMEM((count * GROUP, width), BF16),
            pltpu.VMEM((count * GROUP, filled), BF16),
            pltpu.VMEM((GROUP * patch_count, width), BF16),
            pltpu.VMEM((GROUP * patch_count, GROUP * slots), BF16),
            pltpu.VMEM((groups, GROUP * patch_count, GROUP * slots), BF16),
            pltpu.VMEM((images * heads, width), BF16),
            pltpu.VMEM((RING, images, width), BF16),
            pltpu.VMEM((count // RING, images, width), BF16),
            pltpu.VMEM((RING, images, width), BF16),
            pltpu.VMEM((count // RING, images, width), BF16),
            pltpu.VMEM((RING, images, width), BF16),
            pltpu.VMEM((RING, images, width), BF16),
            pltpu.VMEM((RING, images, width), BF16),
            pltpu.VMEM((RING, images, width), BF16),
            pltpu.SemaphoreType.DMA((images,)),
            pltpu.SemaphoreType.DMA((4,)),
            pltpu.SemaphoreType.DMA((5,)),
            pltpu.SemaphoreType.DMA((10,)),
            pltpu.SemaphoreType.DMA((10,)),
        ],
        compiler_params=pltpu.CompilerParams(
            collective_id=0, has_side_effects=True, vmem_limit_bytes=VMEM_BYTES
        ),
        cost_estimate=pl.CostEstimate(flops=12_000_000_000, bytes_accessed=40_000_000, transcendentals=4_000_000),
    )(
        patches, norm_gain, router, jnp.swapaxes(expert_in, 1, 2), expert_out, post_gain, key_query, value_proj,
        out_proj, text_embed, inverse_heat_exponent, score_intercept,
    )
    return pl.pallas_call(
        unstack,
        out_shape=(out, out, out),
        in_specs=[hbm],
        out_specs=(hbm, hbm, hbm),
        scratch_shapes=[pltpu.SemaphoreType.DMA((3,))],
        compiler_params=pltpu.CompilerParams(vmem_limit_bytes=VMEM_BYTES),
    )(result)


def solution(mesh):
    split = ("dp", "expert")
    placed = (
        P(split, None, None), P(), P(), P(split, None, None), P(split, None, None), P(), P(), P(), P(),
        P(split, None), P(), P(),
    )
    return jax.shard_map(
        body, mesh=mesh, in_specs=placed,
        out_specs=(P(split, None), P(split, None), P(split, None)), check_vma=False,
    )
```

```python
import functools

import jax
import jax.numpy as jnp
from jax import lax
from jax.experimental import pallas as pl
from jax.experimental.pallas import tpu as pltpu
from jax.sharding import PartitionSpec as P

MESH = pl.DeviceIdType.MESH
BF16, F32 = jnp.bfloat16, jnp.float32
BY_ROWS = (((1,), (1,)), ((), ()))
BY_COLUMNS = (((0,), (0,)), ((), ()))
EPS = 1e-6
GROUP = 2
STRIDE = 37
RING = 8
HIDDEN_STEP = 4352
VMEM_BYTES = 60 * 1024 * 1024


def dot(a, b, dims=None):
    if dims is None:
        return jnp.dot(a, b, preferred_element_type=F32)
    return lax.dot_general(a, b, dims, preferred_element_type=F32)


def layer_norm(inputs, gain):
    center = jnp.mean(inputs, axis=1, keepdims=True)
    shifted = inputs - center
    spread = jnp.mean(shifted * shifted, axis=1, keepdims=True)
    return shifted * lax.rsqrt(spread + EPS) * gain


def norm_of(rows):
    return jnp.sqrt(jnp.sum(rows * rows, axis=1, keepdims=True) + EPS)


def split_dot(rows, table, dims=None):
    high = rows.astype(BF16)
    low = (rows - high.astype(F32)).astype(BF16)
    both = dot(jnp.concatenate([high.astype(F32), low.astype(F32)], axis=0).astype(BF16), table, dims)
    return both[: rows.shape[0]] + both[rows.shape[0] :]


def iota(shape, axis):
    return lax.broadcasted_iota(jnp.int32, shape, axis)


def kernel(
    patches_hbm, norm_gain_hbm, router_hbm, in_hbm, out_hbm, post_gain_hbm, query_hbm, value_hbm, proj_hbm,
    text_hbm, heat_ref, intercept_ref,
    result_ref,
    norm_gain_ref, router_ref, post_gain_ref, query_ref, text_ref,
    patches, w_in, w_out, w_value, w_proj,
    sent, rows, answers, returned, expert_x, hidden, normed_buf, dispatch_buf, combine_buf, headed,
    line_texts, texts, line_units, units, image_parts, image_sums, text_parts, text_sums,
    patch_sem, weight_sem, small_sem, send_sem, recv_sem,
):
    expert_size = lax.axis_size("expert")
    count = lax.axis_size("dp") * expert_size
    lines = count // RING
    me = lax.axis_index("dp") * expert_size + lax.axis_index("expert")
    line, spot = me // RING, lax.rem(me, RING)
    images, patch_count, width = patches.shape
    slots = router_ref.shape[1]
    heads = query_ref.shape[0]
    groups = images // GROUP

    def place(target):
        return (target // expert_size, lax.rem(target, expert_size))

    patch_copies = [
        pltpu.make_async_copy(patches_hbm.at[i], patches.at[i], patch_sem.at[i]) for i in range(images)
    ]
    inner_rows = pl.ds(0, in_hbm.shape[1])
    weight_copies = [
        pltpu.make_async_copy(source, target, weight_sem.at[n])
        for n, (source, target) in enumerate(
            [(in_hbm.at[0], w_in.at[inner_rows]), (out_hbm.at[0], w_out.at[inner_rows]), (value_hbm, w_value), (proj_hbm, w_proj)]
        )
    ]
    small_copies = [
        pltpu.make_async_copy(source, target, small_sem.at[n])
        for n, (source, target) in enumerate(
            [
                (norm_gain_hbm, norm_gain_ref), (router_hbm, router_ref), (post_gain_hbm, post_gain_ref),
                (query_hbm, query_ref), (text_hbm, text_ref),
            ]
        )
    ]
    for copy in patch_copies[:1] + small_copies + patch_copies[1:]:
        copy.start()
    for copy in weight_copies:
        copy.start(priority=1)

    barrier = pltpu.get_barrier_semaphore()

    @pl.loop(1, count)
    def _(k):
        pl.semaphore_signal(barrier, inc=1, device_id=place(lax.rem(me + k, count)), device_id_type=MESH)

    def to_all(source, target, n):
        @pl.loop(1, count)
        def _(k):
            to = lax.rem(me + k * STRIDE, count)
            pltpu.make_async_remote_copy(
                src_ref=source.at[to], dst_ref=target.at[me], send_sem=send_sem.at[n], recv_sem=recv_sem.at[n],
                device_id=place(to), device_id_type=MESH,
            ).start()

        pltpu.make_async_copy(source.at[me], target.at[me], recv_sem.at[n]).start()

    def have_left(buffer, n):
        part = buffer.at[pl.ds(0, buffer.shape[0] - 1)]
        pltpu.make_async_copy(part, part, send_sem.at[n]).wait()

    def from_all(target, n):
        pltpu.make_async_copy(target, target, recv_sem.at[n]).wait()

    def to_line(source, target, n):
        @pl.loop(1, RING)
        def _(k):
            to = lax.rem(spot + k, RING)
            pltpu.make_async_remote_copy(
                src_ref=source.at[to] if len(source.shape) == 3 else source, dst_ref=target.at[spot],
                send_sem=send_sem.at[n], recv_sem=recv_sem.at[n],
                device_id=place(line * RING + to), device_id_type=MESH,
            ).start()

    def to_lines(table, n):
        @pl.loop(1, lines)
        def _(k):
            to = lax.rem(line + k * 5, lines)
            pltpu.make_async_remote_copy(
                src_ref=table.at[line], dst_ref=table.at[line], send_sem=send_sem.at[n], recv_sem=recv_sem.at[n],
                device_id=place(to * RING + spot), device_id_type=MESH,
            ).start()

    def from_others(table, n):
        part = table.at[pl.ds(0, table.shape[0] - 1)]
        pltpu.make_async_copy(part, part, recv_sem.at[n]).wait()

    for copy in small_copies:
        copy.wait()
    norm_gain = norm_gain_ref[...].astype(F32).reshape(1, width)
    post_gain = post_gain_ref[...].astype(F32).reshape(1, width)

    def patch_wait(image):
        pltpu.make_async_copy(patches_hbm.at[image], patches.at[image], patch_sem.at[image]).wait()

    def spreading(i):
        shape = (slots, GROUP * slots)
        return (iota(shape, 1) == GROUP * iota(shape, 0) + i).astype(F32).astype(BF16)

    def block_of(i):
        return pl.ds(pl.multiple_of(i * patch_count, patch_count), patch_count)

    def dispatch(group):
        @pl.loop(0, GROUP)
        def _(i):
            image = group * GROUP + i
            block = block_of(i)
            patch_wait(image)
            normed = layer_norm(patches[image].astype(F32), norm_gain).astype(BF16)
            normed_buf[block, :] = normed
            logits = dot(normed, router_ref[...])
            spread = spreading(i)
            weighted = jnp.exp(logits - jnp.max(logits, axis=0, keepdims=True))
            weighted = (weighted / jnp.sum(weighted, axis=0, keepdims=True)).astype(BF16)
            dispatch_buf[block, :] = dot(weighted, spread).astype(BF16)
            mixing = jnp.exp(logits - jnp.max(logits, axis=1, keepdims=True))
            mixing = (mixing / jnp.sum(mixing, axis=1, keepdims=True)).astype(BF16)
            combine_buf[group, block, :] = dot(mixing, spread).astype(BF16)

        slot_in = dot(dispatch_buf[...], normed_buf[...], BY_COLUMNS).astype(BF16)
        sent[group] = slot_in.reshape(slots, GROUP, width)

    def experts(group):
        expert_x[...] = rows[group].reshape(count * GROUP, width)

        @pl.loop(0, hidden.shape[1] // HIDDEN_STEP)
        def _(k):
            part = pl.ds(pl.multiple_of(k * HIDDEN_STEP, HIDDEN_STEP), HIDDEN_STEP)
            pre = dot(expert_x[...], w_in[part, :], BY_ROWS)
            hidden[:, part] = jax.nn.gelu(pre, approximate=True).astype(BF16)

        answers[group] = dot(hidden[...], w_out[...]).astype(BF16).reshape(count, GROUP, width)

    def pool(group):
        for i in range(GROUP):
            image = group * GROUP + i
            slot_out = returned[group].reshape(slots * GROUP, width)
            mixed = patches[image].astype(F32) + dot(combine_buf[group, pl.ds(i * patch_count, patch_count), :], slot_out)
            pool_in = layer_norm(mixed, post_gain).astype(BF16)
            scores = dot(query_ref[...], pool_in, BY_ROWS)
            attend = jnp.exp(scores - jnp.max(scores, axis=1, keepdims=True))
            mass = jnp.sum(attend, axis=1, keepdims=True)
            summed = dot(attend.astype(BF16), pool_in) / mass
            headed[pl.ds(pl.multiple_of(image * heads, heads), heads), :] = summed.astype(BF16)

    inner = in_hbm.shape[1]
    filler = w_in.shape[0] - inner
    w_in[pl.ds(inner, filler), :] = jnp.zeros((filler, width), BF16)
    w_out[pl.ds(inner, filler), :] = jnp.zeros((filler, width), BF16)

    @pl.loop(0, groups)
    def _(group):
        dispatch(group)

        @pl.when(group == 0)
        def _():
            pl.semaphore_wait(barrier, count - 1)

        @pl.when(group > 0)
        def _():
            have_left(sent.at[0], 0)

        to_all(sent.at[group], rows.at[group], group)

    weight_copies[0].wait()
    weight_copies[1].wait()

    @pl.loop(0, groups)
    def _(group):
        from_all(rows.at[group], group)
        experts(group)
        to_all(answers.at[group], returned.at[group], groups + group)

        @pl.when(group == 0)
        def _():
            line_texts[spot] = text_ref[...]
            texts[line] = text_ref[...]
            to_line(line_texts.at[spot], line_texts, 4)
            to_lines(texts, 5)

    text = text_ref[...]
    weight_copies[2].wait()
    weight_copies[3].wait()

    @pl.loop(0, groups)
    def _(group):
        from_all(returned.at[group], groups + group)
        pool(group)

    full = dot(headed[...], w_value[...])
    head_width = width // heads
    head = lax.rem(iota(full.shape, 0), heads)
    column = iota(full.shape, 1)
    own_head = (column >= head * head_width) & (column < (head + 1) * head_width)
    values = jnp.sum(jnp.where(own_head, full, 0.0).reshape(images, heads, width), axis=1)
    pooled = dot(values.astype(BF16), w_proj[...])
    result_ref[0] = pooled
    img_norm = norm_of(pooled)
    unit = pooled / img_norm
    line_units[spot] = unit.astype(BF16)
    units[line] = unit.astype(BF16)
    to_line(line_units.at[spot], line_units, 6)
    to_lines(units, 7)

    heat = jnp.exp(jnp.full((1, 1), heat_ref[0], F32))
    intercept = intercept_ref[0]
    pairs = images * count
    near, far = images * RING, images * lines
    row, col = iota((near, far), 0), iota((near, far), 1)
    own_row = (row >= spot * images) & (row < (spot + 1) * images)
    label = jnp.where(own_row & (row - spot * images == col - line * images), 1.0, -1.0)

    zeros = jnp.zeros((images, width), BF16)
    image_sums[spot] = zeros
    text_sums[spot] = zeros

    def own_block(part):
        return jnp.sum(jnp.where(own_row[:, 0:1], part, 0.0).reshape(RING, images, width), axis=0)

    def coefficients(cosines):
        scores = heat * cosines + intercept
        return -label * jax.nn.sigmoid(-label * scores) / pairs

    from_others(line_texts, 4)
    from_others(texts, 5)
    table = texts[...].reshape(far, width)
    table_norm = norm_of(table.astype(F32))
    table_norm = jnp.transpose(jnp.broadcast_to(table_norm, (far, 128)))[0:1, :]
    near_texts = line_texts[...].reshape(near, width)
    near_norms = norm_of(near_texts.astype(F32))
    text = text.astype(F32)
    text_norm = norm_of(text)
    unit_text = text / text_norm
    from_others(line_units, 6)
    cosines = dot(line_units[...].reshape(near, width), table, BY_ROWS) / table_norm
    part = heat * split_dot(coefficients(cosines) / table_norm, table)
    image_parts[...] = part.astype(BF16).reshape(RING, images, width)
    to_line(image_parts, image_sums, 8)
    own_image_part = own_block(part)

    from_others(units, 7)
    table = units[...].reshape(far, width)
    cosines = dot(near_texts, table, BY_ROWS) / near_norms
    part = heat * split_dot(coefficients(cosines), table)
    text_parts[...] = part.astype(BF16).reshape(RING, images, width)
    to_line(text_parts, text_sums, 9)
    own_text_part = own_block(part)

    from_others(image_sums, 8)
    grad = own_image_part + jnp.sum(image_sums[...].astype(F32), axis=0)
    result_ref[1] = (grad - unit * jnp.sum(unit * grad, axis=1, keepdims=True)) / img_norm
    from_others(text_sums, 9)
    grad = own_text_part + jnp.sum(text_sums[...].astype(F32), axis=0)
    result_ref[2] = (grad - unit_text * jnp.sum(unit_text * grad, axis=1, keepdims=True)) / text_norm

    blocks = [
        sent.at[1], answers.at[0], answers.at[1], line_texts, texts, line_units, units, image_parts, text_parts,
    ]
    for n, buffer in enumerate(blocks):
        have_left(buffer, n + 1)


def unstack(stacked_ref, pooled_ref, pooled_grad_ref, text_grad_ref, sem):
    copies = [
        pltpu.make_async_copy(stacked_ref.at[n], target, sem.at[n])
        for n, target in enumerate((pooled_ref, pooled_grad_ref, text_grad_ref))
    ]
    for copy in copies:
        copy.start()
    for copy in copies:
        copy.wait()


def body(
    patches, norm_gain, router, expert_in, expert_out, post_gain, key_query, value_proj, out_proj, text_embed,
    inverse_heat_exponent, score_intercept,
):
    images, patch_count, width = patches.shape
    inner = expert_out.shape[1]
    slots, heads = router.shape[1], key_query.shape[0]
    count = lax.axis_size("dp") * lax.axis_size("expert")
    groups = images // GROUP
    vmem = pl.BlockSpec(memory_space=pltpu.VMEM)
    hbm = pl.BlockSpec(memory_space=pl.ANY)
    filled = -(-inner // HIDDEN_STEP) * HIDDEN_STEP
    traffic = (groups, count, GROUP, width)
    out = jax.ShapeDtypeStruct((images, width), F32)
    result = pl.pallas_call(
        kernel,
        out_shape=jax.ShapeDtypeStruct((3, images, width), F32),
        in_specs=[hbm] * 10 + [pl.BlockSpec(memory_space=pltpu.SMEM)] * 2,
        out_specs=vmem,
        scratch_shapes=[
            pltpu.VMEM((width,), BF16),
            pltpu.VMEM(router.shape, BF16),
            pltpu.VMEM((width,), BF16),
            pltpu.VMEM(key_query.shape, BF16),
            pltpu.VMEM(text_embed.shape, BF16),
            pltpu.VMEM(patches.shape, BF16),
            pltpu.VMEM((filled, width), BF16),
            pltpu.VMEM((filled, width), BF16),
            pltpu.VMEM(value_proj.shape, BF16),
            pltpu.VMEM(out_proj.shape, BF16),
            pltpu.VMEM(traffic, BF16),
            pltpu.VMEM(traffic, BF16),
            pltpu.VMEM(traffic, BF16),
            pltpu.VMEM(traffic, BF16),
            pltpu.VMEM((count * GROUP, width), BF16),
            pltpu.VMEM((count * GROUP, filled), BF16),
            pltpu.VMEM((GROUP * patch_count, width), BF16),
            pltpu.VMEM((GROUP * patch_count, GROUP * slots), BF16),
            pltpu.VMEM((groups, GROUP * patch_count, GROUP * slots), BF16),
            pltpu.VMEM((images * heads, width), BF16),
            pltpu.VMEM((RING, images, width), BF16),
            pltpu.VMEM((count // RING, images, width), BF16),
            pltpu.VMEM((RING, images, width), BF16),
            pltpu.VMEM((count // RING, images, width), BF16),
            pltpu.VMEM((RING, images, width), BF16),
            pltpu.VMEM((RING, images, width), BF16),
            pltpu.VMEM((RING, images, width), BF16),
            pltpu.VMEM((RING, images, width), BF16),
            pltpu.SemaphoreType.DMA((images,)),
            pltpu.SemaphoreType.DMA((4,)),
            pltpu.SemaphoreType.DMA((5,)),
            pltpu.SemaphoreType.DMA((10,)),
            pltpu.SemaphoreType.DMA((10,)),
        ],
        compiler_params=pltpu.CompilerParams(
            collective_id=0, has_side_effects=True, vmem_limit_bytes=VMEM_BYTES
        ),
        cost_estimate=pl.CostEstimate(flops=12_000_000_000, bytes_accessed=40_000_000, transcendentals=4_000_000),
    )(
        patches, norm_gain, router, jnp.swapaxes(expert_in, 1, 2), expert_out, post_gain, key_query, value_proj,
        out_proj, text_embed, inverse_heat_exponent, score_intercept,
    )
    return pl.pallas_call(
        unstack,
        out_shape=(out, out, out),
        in_specs=[hbm],
        out_specs=(hbm, hbm, hbm),
        scratch_shapes=[pltpu.SemaphoreType.DMA((3,))],
        compiler_params=pltpu.CompilerParams(vmem_limit_bytes=VMEM_BYTES),
    )(result)


def solution(mesh):
    split = ("dp", "expert")
    placed = (
        P(split, None, None), P(), P(), P(split, None, None), P(split, None, None), P(), P(), P(), P(),
        P(split, None), P(), P(),
    )
    return jax.shard_map(
        body, mesh=mesh, in_specs=placed,
        out_specs=(P(split, None), P(split, None), P(split, None)), check_vma=False,
    )
```

```python
import functools

import jax
import jax.numpy as jnp
from jax import lax
from jax.experimental import pallas as pl
from jax.experimental.pallas import tpu as pltpu
from jax.sharding import PartitionSpec as P

MESH = pl.DeviceIdType.MESH
BF16, F32 = jnp.bfloat16, jnp.float32
BY_ROWS = (((1,), (1,)), ((), ()))
BY_COLUMNS = (((0,), (0,)), ((), ()))
EPS = 1e-6
GROUP = 2
STRIDE = 37
SEND_BATCH = 14
RING = 8
HIDDEN_STEP = 4352
VMEM_BYTES = 60 * 1024 * 1024


def dot(a, b, dims=None):
    if dims is None:
        return jnp.dot(a, b, preferred_element_type=F32)
    return lax.dot_general(a, b, dims, preferred_element_type=F32)


def layer_norm(inputs, gain):
    center = jnp.mean(inputs, axis=1, keepdims=True)
    shifted = inputs - center
    spread = jnp.mean(shifted * shifted, axis=1, keepdims=True)
    return shifted * lax.rsqrt(spread + EPS) * gain


def norm_of(rows):
    return jnp.sqrt(jnp.sum(rows * rows, axis=1, keepdims=True) + EPS)


def split_dot(rows, table, dims=None):
    high = rows.astype(BF16)
    low = (rows - high.astype(F32)).astype(BF16)
    both = dot(jnp.concatenate([high.astype(F32), low.astype(F32)], axis=0).astype(BF16), table, dims)
    return both[: rows.shape[0]] + both[rows.shape[0] :]


def iota(shape, axis):
    return lax.broadcasted_iota(jnp.int32, shape, axis)


def kernel(
    patches_hbm, norm_gain_hbm, router_hbm, in_hbm, out_hbm, post_gain_hbm, query_hbm, value_hbm, proj_hbm,
    text_hbm, heat_ref, intercept_ref,
    result_ref,
    norm_gain_ref, router_ref, post_gain_ref, query_ref, text_ref,
    patches, w_in, w_out, w_value, w_proj,
    sent, rows, answers, returned, expert_x, hidden, normed_buf, dispatch_buf, combine_buf, headed,
    line_texts, texts, line_units, units, image_parts, image_sums, text_parts, text_sums,
    patch_sem, weight_sem, small_sem, send_sem, recv_sem,
):
    expert_size = lax.axis_size("expert")
    count = lax.axis_size("dp") * expert_size
    lines = count // RING
    me = lax.axis_index("dp") * expert_size + lax.axis_index("expert")
    line, spot = me // RING, lax.rem(me, RING)
    images, patch_count, width = patches.shape
    slots = router_ref.shape[1]
    heads = query_ref.shape[0]
    groups = images // GROUP

    def place(target):
        return (target // expert_size, lax.rem(target, expert_size))

    patch_copies = [
        pltpu.make_async_copy(patches_hbm.at[i], patches.at[i], patch_sem.at[i]) for i in range(images)
    ]
    inner_rows = pl.ds(0, in_hbm.shape[1])
    weight_copies = [
        pltpu.make_async_copy(source, target, weight_sem.at[n])
        for n, (source, target) in enumerate(
            [(in_hbm.at[0], w_in.at[inner_rows]), (out_hbm.at[0], w_out.at[inner_rows]), (value_hbm, w_value), (proj_hbm, w_proj)]
        )
    ]
    small_copies = [
        pltpu.make_async_copy(source, target, small_sem.at[n])
        for n, (source, target) in enumerate(
            [
                (norm_gain_hbm, norm_gain_ref), (router_hbm, router_ref), (post_gain_hbm, post_gain_ref),
                (query_hbm, query_ref), (text_hbm, text_ref),
            ]
        )
    ]
    for copy in patch_copies[:1] + small_copies + patch_copies[1:]:
        copy.start()
    for copy in weight_copies:
        copy.start(priority=1)

    barrier = pltpu.get_barrier_semaphore()

    @pl.loop(1, count)
    def _(k):
        pl.semaphore_signal(barrier, inc=1, device_id=place(lax.rem(me + k, count)), device_id_type=MESH)

    def to_all(source, target, n):
        def send(k):
            to = lax.rem(me + k * STRIDE, count)
            pltpu.make_async_remote_copy(
                src_ref=source.at[to], dst_ref=target.at[me], send_sem=send_sem.at[n], recv_sem=recv_sem.at[n],
                device_id=place(to), device_id_type=MESH,
            ).start()

        batches = (count - 1) // SEND_BATCH

        @pl.loop(0, batches)
        def _(batch):
            for k in range(SEND_BATCH):
                send(batch * SEND_BATCH + k + 1)

        for k in range(batches * SEND_BATCH + 1, count):
            send(k)

        pltpu.make_async_copy(source.at[me], target.at[me], recv_sem.at[n]).start()

    def have_left(buffer, n):
        part = buffer.at[pl.ds(0, buffer.shape[0] - 1)]
        pltpu.make_async_copy(part, part, send_sem.at[n]).wait()

    def from_all(target, n):
        pltpu.make_async_copy(target, target, recv_sem.at[n]).wait()

    def to_line(source, target, n):
        @pl.loop(1, RING)
        def _(k):
            to = lax.rem(spot + k, RING)
            pltpu.make_async_remote_copy(
                src_ref=source.at[to] if len(source.shape) == 3 else source, dst_ref=target.at[spot],
                send_sem=send_sem.at[n], recv_sem=recv_sem.at[n],
                device_id=place(line * RING + to), device_id_type=MESH,
            ).start()

    def to_lines(table, n):
        @pl.loop(1, lines)
        def _(k):
            to = lax.rem(line + k * 5, lines)
            pltpu.make_async_remote_copy(
                src_ref=table.at[line], dst_ref=table.at[line], send_sem=send_sem.at[n], recv_sem=recv_sem.at[n],
                device_id=place(to * RING + spot), device_id_type=MESH,
            ).start()

    def from_others(table, n):
        part = table.at[pl.ds(0, table.shape[0] - 1)]
        pltpu.make_async_copy(part, part, recv_sem.at[n]).wait()

    for copy in small_copies:
        copy.wait()
    norm_gain = norm_gain_ref[...].astype(F32).reshape(1, width)
    post_gain = post_gain_ref[...].astype(F32).reshape(1, width)

    def patch_wait(image):
        pltpu.make_async_copy(patches_hbm.at[image], patches.at[image], patch_sem.at[image]).wait()

    def spreading(i):
        shape = (slots, GROUP * slots)
        return (iota(shape, 1) == GROUP * iota(shape, 0) + i).astype(F32).astype(BF16)

    def block_of(i):
        return pl.ds(pl.multiple_of(i * patch_count, patch_count), patch_count)

    def dispatch(group):
        @pl.loop(0, GROUP)
        def _(i):
            image = group * GROUP + i
            block = block_of(i)
            patch_wait(image)
            normed = layer_norm(patches[image].astype(F32), norm_gain).astype(BF16)
            normed_buf[block, :] = normed
            logits = dot(normed, router_ref[...])
            spread = spreading(i)
            weighted = jnp.exp(logits - jnp.max(logits, axis=0, keepdims=True))
            weighted = (weighted / jnp.sum(weighted, axis=0, keepdims=True)).astype(BF16)
            dispatch_buf[block, :] = dot(weighted, spread).astype(BF16)
            mixing = jnp.exp(logits - jnp.max(logits, axis=1, keepdims=True))
            mixing = (mixing / jnp.sum(mixing, axis=1, keepdims=True)).astype(BF16)
            combine_buf[group, block, :] = dot(mixing, spread).astype(BF16)

        slot_in = dot(dispatch_buf[...], normed_buf[...], BY_COLUMNS).astype(BF16)
        sent[group] = slot_in.reshape(slots, GROUP, width)

    def experts(group):
        expert_x[...] = rows[group].reshape(count * GROUP, width)

        @pl.loop(0, hidden.shape[1] // HIDDEN_STEP)
        def _(k):
            part = pl.ds(pl.multiple_of(k * HIDDEN_STEP, HIDDEN_STEP), HIDDEN_STEP)
            pre = dot(expert_x[...], w_in[part, :], BY_ROWS)
            hidden[:, part] = jax.nn.gelu(pre, approximate=True).astype(BF16)

        answers[group] = dot(hidden[...], w_out[...]).astype(BF16).reshape(count, GROUP, width)

    def pool(group):
        for i in range(GROUP):
            image = group * GROUP + i
            slot_out = returned[group].reshape(slots * GROUP, width)
            mixed = patches[image].astype(F32) + dot(combine_buf[group, pl.ds(i * patch_count, patch_count), :], slot_out)
            pool_in = layer_norm(mixed, post_gain).astype(BF16)
            scores = dot(query_ref[...], pool_in, BY_ROWS)
            attend = jnp.exp(scores - jnp.max(scores, axis=1, keepdims=True))
            mass = jnp.sum(attend, axis=1, keepdims=True)
            summed = dot(attend.astype(BF16), pool_in) / mass
            headed[pl.ds(pl.multiple_of(image * heads, heads), heads), :] = summed.astype(BF16)

    inner = in_hbm.shape[1]
    filler = w_in.shape[0] - inner
    w_in[pl.ds(inner, filler), :] = jnp.zeros((filler, width), BF16)
    w_out[pl.ds(inner, filler), :] = jnp.zeros((filler, width), BF16)

    @pl.loop(0, groups)
    def _(group):
        dispatch(group)

        @pl.when(group == 0)
        def _():
            pl.semaphore_wait(barrier, count - 1)

        @pl.when(group > 0)
        def _():
            have_left(sent.at[0], 0)

        to_all(sent.at[group], rows.at[group], group)

    weight_copies[0].wait()
    weight_copies[1].wait()

    @pl.loop(0, groups)
    def _(group):
        from_all(rows.at[group], group)
        experts(group)
        to_all(answers.at[group], returned.at[group], groups + group)

        @pl.when(group == 0)
        def _():
            line_texts[spot] = text_ref[...]
            texts[line] = text_ref[...]
            to_line(line_texts.at[spot], line_texts, 4)
            to_lines(texts, 5)

    text = text_ref[...]
    weight_copies[2].wait()
    weight_copies[3].wait()

    @pl.loop(0, groups)
    def _(group):
        from_all(returned.at[group], groups + group)
        pool(group)

    full = dot(headed[...], w_value[...])
    head_width = width // heads
    head = lax.rem(iota(full.shape, 0), heads)
    column = iota(full.shape, 1)
    own_head = (column >= head * head_width) & (column < (head + 1) * head_width)
    values = jnp.sum(jnp.where(own_head, full, 0.0).reshape(images, heads, width), axis=1)
    pooled = dot(values.astype(BF16), w_proj[...])
    result_ref[0] = pooled
    img_norm = norm_of(pooled)
    unit = pooled / img_norm
    line_units[spot] = unit.astype(BF16)
    units[line] = unit.astype(BF16)
    to_line(line_units.at[spot], line_units, 6)
    to_lines(units, 7)

    heat = jnp.exp(jnp.full((1, 1), heat_ref[0], F32))
    intercept = intercept_ref[0]
    pairs = images * count
    near, far = images * RING, images * lines
    row, col = iota((near, far), 0), iota((near, far), 1)
    own_row = (row >= spot * images) & (row < (spot + 1) * images)
    label = jnp.where(own_row & (row - spot * images == col - line * images), 1.0, -1.0)

    zeros = jnp.zeros((images, width), BF16)
    image_sums[spot] = zeros
    text_sums[spot] = zeros

    def own_block(part):
        return jnp.sum(jnp.where(own_row[:, 0:1], part, 0.0).reshape(RING, images, width), axis=0)

    def coefficients(cosines):
        scores = heat * cosines + intercept
        return -label * jax.nn.sigmoid(-label * scores) / pairs

    from_others(line_texts, 4)
    from_others(texts, 5)
    table = texts[...].reshape(far, width)
    table_norm = norm_of(table.astype(F32))
    table_norm = jnp.transpose(jnp.broadcast_to(table_norm, (far, 128)))[0:1, :]
    near_texts = line_texts[...].reshape(near, width)
    near_norms = norm_of(near_texts.astype(F32))
    text = text.astype(F32)
    text_norm = norm_of(text)
    unit_text = text / text_norm
    from_others(line_units, 6)
    cosines = dot(line_units[...].reshape(near, width), table, BY_ROWS) / table_norm
    part = heat * split_dot(coefficients(cosines) / table_norm, table)
    image_parts[...] = part.astype(BF16).reshape(RING, images, width)
    to_line(image_parts, image_sums, 8)
    own_image_part = own_block(part)

    from_others(units, 7)
    table = units[...].reshape(far, width)
    cosines = dot(near_texts, table, BY_ROWS) / near_norms
    part = heat * split_dot(coefficients(cosines), table)
    text_parts[...] = part.astype(BF16).reshape(RING, images, width)
    to_line(text_parts, text_sums, 9)
    own_text_part = own_block(part)

    from_others(image_sums, 8)
    grad = own_image_part + jnp.sum(image_sums[...].astype(F32), axis=0)
    result_ref[1] = (grad - unit * jnp.sum(unit * grad, axis=1, keepdims=True)) / img_norm
    from_others(text_sums, 9)
    grad = own_text_part + jnp.sum(text_sums[...].astype(F32), axis=0)
    result_ref[2] = (grad - unit_text * jnp.sum(unit_text * grad, axis=1, keepdims=True)) / text_norm

    blocks = [
        sent.at[1], answers.at[0], answers.at[1], line_texts, texts, line_units, units, image_parts, text_parts,
    ]
    for n, buffer in enumerate(blocks):
        have_left(buffer, n + 1)


def unstack(stacked_ref, pooled_ref, pooled_grad_ref, text_grad_ref, sem):
    copies = [
        pltpu.make_async_copy(stacked_ref.at[n], target, sem.at[n])
        for n, target in enumerate((pooled_ref, pooled_grad_ref, text_grad_ref))
    ]
    for copy in copies:
        copy.start()
    for copy in copies:
        copy.wait()


def body(
    patches, norm_gain, router, expert_in, expert_out, post_gain, key_query, value_proj, out_proj, text_embed,
    inverse_heat_exponent, score_intercept,
):
    images, patch_count, width = patches.shape
    inner = expert_out.shape[1]
    slots, heads = router.shape[1], key_query.shape[0]
    count = lax.axis_size("dp") * lax.axis_size("expert")
    groups = images // GROUP
    vmem = pl.BlockSpec(memory_space=pltpu.VMEM)
    hbm = pl.BlockSpec(memory_space=pl.ANY)
    filled = -(-inner // HIDDEN_STEP) * HIDDEN_STEP
    traffic = (groups, count, GROUP, width)
    out = jax.ShapeDtypeStruct((images, width), F32)
    result = pl.pallas_call(
        kernel,
        out_shape=jax.ShapeDtypeStruct((3, images, width), F32),
        in_specs=[hbm] * 10 + [pl.BlockSpec(memory_space=pltpu.SMEM)] * 2,
        out_specs=vmem,
        scratch_shapes=[
            pltpu.VMEM((width,), BF16),
            pltpu.VMEM(router.shape, BF16),
            pltpu.VMEM((width,), BF16),
            pltpu.VMEM(key_query.shape, BF16),
            pltpu.VMEM(text_embed.shape, BF16),
            pltpu.VMEM(patches.shape, BF16),
            pltpu.VMEM((filled, width), BF16),
            pltpu.VMEM((filled, width), BF16),
            pltpu.VMEM(value_proj.shape, BF16),
            pltpu.VMEM(out_proj.shape, BF16),
            pltpu.VMEM(traffic, BF16),
            pltpu.VMEM(traffic, BF16),
            pltpu.VMEM(traffic, BF16),
            pltpu.VMEM(traffic, BF16),
            pltpu.VMEM((count * GROUP, width), BF16),
            pltpu.VMEM((count * GROUP, filled), BF16),
            pltpu.VMEM((GROUP * patch_count, width), BF16),
            pltpu.VMEM((GROUP * patch_count, GROUP * slots), BF16),
            pltpu.VMEM((groups, GROUP * patch_count, GROUP * slots), BF16),
            pltpu.VMEM((images * heads, width), BF16),
            pltpu.VMEM((RING, images, width), BF16),
            pltpu.VMEM((count // RING, images, width), BF16),
            pltpu.VMEM((RING, images, width), BF16),
            pltpu.VMEM((count // RING, images, width), BF16),
            pltpu.VMEM((RING, images, width), BF16),
            pltpu.VMEM((RING, images, width), BF16),
            pltpu.VMEM((RING, images, width), BF16),
            pltpu.VMEM((RING, images, width), BF16),
            pltpu.SemaphoreType.DMA((images,)),
            pltpu.SemaphoreType.DMA((4,)),
            pltpu.SemaphoreType.DMA((5,)),
            pltpu.SemaphoreType.DMA((10,)),
            pltpu.SemaphoreType.DMA((10,)),
        ],
        compiler_params=pltpu.CompilerParams(
            collective_id=0, has_side_effects=True, vmem_limit_bytes=VMEM_BYTES
        ),
        cost_estimate=pl.CostEstimate(flops=12_000_000_000, bytes_accessed=40_000_000, transcendentals=4_000_000),
    )(
        patches, norm_gain, router, jnp.swapaxes(expert_in, 1, 2), expert_out, post_gain, key_query, value_proj,
        out_proj, text_embed, inverse_heat_exponent, score_intercept,
    )
    return pl.pallas_call(
        unstack,
        out_shape=(out, out, out),
        in_specs=[hbm],
        out_specs=(hbm, hbm, hbm),
        scratch_shapes=[pltpu.SemaphoreType.DMA((3,))],
        compiler_params=pltpu.CompilerParams(vmem_limit_bytes=VMEM_BYTES),
    )(result)


def solution(mesh):
    split = ("dp", "expert")
    placed = (
        P(split, None, None), P(), P(), P(split, None, None), P(split, None, None), P(), P(), P(), P(),
        P(split, None), P(), P(),
    )
    return jax.shard_map(
        body, mesh=mesh, in_specs=placed,
        out_specs=(P(split, None), P(split, None), P(split, None)), check_vma=False,
    )
```

```python
import functools

import jax
import jax.numpy as jnp
from jax import lax
from jax.experimental import pallas as pl
from jax.experimental.pallas import tpu as pltpu
from jax.sharding import PartitionSpec as P

MESH = pl.DeviceIdType.MESH
BF16, F32 = jnp.bfloat16, jnp.float32
BY_ROWS = (((1,), (1,)), ((), ()))
BY_COLUMNS = (((0,), (0,)), ((), ()))
EPS = 1e-6
GROUP = 2
STRIDE = 37
SEND_BATCH = 14
RING = 8
HIDDEN_STEP = 4352
VMEM_BYTES = 60 * 1024 * 1024


def dot(a, b, dims=None):
    if dims is None:
        return jnp.dot(a, b, preferred_element_type=F32)
    return lax.dot_general(a, b, dims, preferred_element_type=F32)


def layer_norm(inputs, gain):
    center = jnp.mean(inputs, axis=1, keepdims=True)
    shifted = inputs - center
    spread = jnp.mean(shifted * shifted, axis=1, keepdims=True)
    return shifted * lax.rsqrt(spread + EPS) * gain


def norm_of(rows):
    return jnp.sqrt(jnp.sum(rows * rows, axis=1, keepdims=True) + EPS)


def split_dot(rows, table, dims=None):
    high = rows.astype(BF16)
    low = (rows - high.astype(F32)).astype(BF16)
    both = dot(jnp.concatenate([high.astype(F32), low.astype(F32)], axis=0).astype(BF16), table, dims)
    return both[: rows.shape[0]] + both[rows.shape[0] :]


def iota(shape, axis):
    return lax.broadcasted_iota(jnp.int32, shape, axis)


def kernel(
    patches_hbm, norm_gain_hbm, router_hbm, in_hbm, out_hbm, post_gain_hbm, query_hbm, value_hbm, proj_hbm,
    text_hbm, heat_ref, intercept_ref,
    result_ref,
    norm_gain_ref, router_ref, post_gain_ref, query_ref, text_ref,
    patches, w_in, w_out, w_value, w_proj,
    sent, rows, answers, returned, expert_x, hidden, normed_buf, dispatch_buf, combine_buf, headed,
    line_texts, texts, line_units, units, image_parts, image_sums, text_parts, text_sums,
    patch_sem, weight_sem, small_sem, send_sem, recv_sem,
):
    expert_size = lax.axis_size("expert")
    count = lax.axis_size("dp") * expert_size
    lines = count // RING
    me = lax.axis_index("dp") * expert_size + lax.axis_index("expert")
    line, spot = me // RING, lax.rem(me, RING)
    images, patch_count, width = patches.shape
    slots = router_ref.shape[1]
    heads = query_ref.shape[0]
    groups = images // GROUP

    def place(target):
        return (target // expert_size, lax.rem(target, expert_size))

    patch_copies = [
        pltpu.make_async_copy(patches_hbm.at[i], patches.at[i], patch_sem.at[i]) for i in range(images)
    ]
    inner_rows = pl.ds(0, in_hbm.shape[1])
    weight_copies = [
        pltpu.make_async_copy(source, target, weight_sem.at[n])
        for n, (source, target) in enumerate(
            [(in_hbm.at[0], w_in.at[inner_rows]), (out_hbm.at[0], w_out.at[inner_rows]), (value_hbm, w_value), (proj_hbm, w_proj)]
        )
    ]
    small_copies = [
        pltpu.make_async_copy(source, target, small_sem.at[n])
        for n, (source, target) in enumerate(
            [
                (norm_gain_hbm, norm_gain_ref), (router_hbm, router_ref), (post_gain_hbm, post_gain_ref),
                (query_hbm, query_ref), (text_hbm, text_ref),
            ]
        )
    ]
    for copy in patch_copies[:1] + small_copies + patch_copies[1:]:
        copy.start()
    for copy in weight_copies:
        copy.start(priority=1)

    barrier = pltpu.get_barrier_semaphore()

    @pl.loop(1, count)
    def _(k):
        pl.semaphore_signal(barrier, inc=1, device_id=place(lax.rem(me + k, count)), device_id_type=MESH)

    def to_all(source, target, n):
        def send(k):
            to = lax.rem(me + k * STRIDE, count)
            pltpu.make_async_remote_copy(
                src_ref=source.at[to], dst_ref=target.at[me], send_sem=send_sem.at[n], recv_sem=recv_sem.at[n],
                device_id=place(to), device_id_type=MESH,
            ).start()

        batches = (count - 1) // SEND_BATCH

        @pl.loop(0, batches)
        def _(batch):
            for k in range(SEND_BATCH):
                send(batch * SEND_BATCH + k + 1)

        for k in range(batches * SEND_BATCH + 1, count):
            send(k)

        pltpu.make_async_copy(source.at[me], target.at[me], recv_sem.at[n]).start()

    def have_left(buffer, n):
        part = buffer.at[pl.ds(0, buffer.shape[0] - 1)]
        pltpu.make_async_copy(part, part, send_sem.at[n]).wait()

    def from_all(target, n):
        pltpu.make_async_copy(target, target, recv_sem.at[n]).wait()

    def to_line(source, target, n):
        for k in range(1, RING):
            to = lax.rem(spot + k, RING)
            pltpu.make_async_remote_copy(
                src_ref=source.at[to] if len(source.shape) == 3 else source, dst_ref=target.at[spot],
                send_sem=send_sem.at[n], recv_sem=recv_sem.at[n],
                device_id=place(line * RING + to), device_id_type=MESH,
            ).start()

    def to_lines(table, n):
        for k in range(1, lines):
            to = lax.rem(line + k * 5, lines)
            pltpu.make_async_remote_copy(
                src_ref=table.at[line], dst_ref=table.at[line], send_sem=send_sem.at[n], recv_sem=recv_sem.at[n],
                device_id=place(to * RING + spot), device_id_type=MESH,
            ).start()

    def from_others(table, n):
        part = table.at[pl.ds(0, table.shape[0] - 1)]
        pltpu.make_async_copy(part, part, recv_sem.at[n]).wait()

    for copy in small_copies:
        copy.wait()
    norm_gain = norm_gain_ref[...].astype(F32).reshape(1, width)
    post_gain = post_gain_ref[...].astype(F32).reshape(1, width)

    def patch_wait(image):
        pltpu.make_async_copy(patches_hbm.at[image], patches.at[image], patch_sem.at[image]).wait()

    def spreading(i):
        shape = (slots, GROUP * slots)
        return (iota(shape, 1) == GROUP * iota(shape, 0) + i).astype(F32).astype(BF16)

    def block_of(i):
        return pl.ds(pl.multiple_of(i * patch_count, patch_count), patch_count)

    def dispatch(group):
        @pl.loop(0, GROUP)
        def _(i):
            image = group * GROUP + i
            block = block_of(i)
            patch_wait(image)
            normed = layer_norm(patches[image].astype(F32), norm_gain).astype(BF16)
            normed_buf[block, :] = normed
            logits = dot(normed, router_ref[...])
            spread = spreading(i)
            weighted = jnp.exp(logits - jnp.max(logits, axis=0, keepdims=True))
            weighted = (weighted / jnp.sum(weighted, axis=0, keepdims=True)).astype(BF16)
            dispatch_buf[block, :] = dot(weighted, spread).astype(BF16)
            mixing = jnp.exp(logits - jnp.max(logits, axis=1, keepdims=True))
            mixing = (mixing / jnp.sum(mixing, axis=1, keepdims=True)).astype(BF16)
            combine_buf[group, block, :] = dot(mixing, spread).astype(BF16)

        slot_in = dot(dispatch_buf[...], normed_buf[...], BY_COLUMNS).astype(BF16)
        sent[group] = slot_in.reshape(slots, GROUP, width)

    def experts(group):
        expert_x[...] = rows[group].reshape(count * GROUP, width)

        @pl.loop(0, hidden.shape[1] // HIDDEN_STEP)
        def _(k):
            part = pl.ds(pl.multiple_of(k * HIDDEN_STEP, HIDDEN_STEP), HIDDEN_STEP)
            pre = dot(expert_x[...], w_in[part, :], BY_ROWS)
            hidden[:, part] = jax.nn.gelu(pre, approximate=True).astype(BF16)

        answers[group] = dot(hidden[...], w_out[...]).astype(BF16).reshape(count, GROUP, width)

    def pool(group):
        for i in range(GROUP):
            image = group * GROUP + i
            slot_out = returned[group].reshape(slots * GROUP, width)
            mixed = patches[image].astype(F32) + dot(combine_buf[group, pl.ds(i * patch_count, patch_count), :], slot_out)
            pool_in = layer_norm(mixed, post_gain).astype(BF16)
            scores = dot(query_ref[...], pool_in, BY_ROWS)
            attend = jnp.exp(scores - jnp.max(scores, axis=1, keepdims=True))
            mass = jnp.sum(attend, axis=1, keepdims=True)
            summed = dot(attend.astype(BF16), pool_in) / mass
            headed[pl.ds(pl.multiple_of(image * heads, heads), heads), :] = summed.astype(BF16)

    inner = in_hbm.shape[1]
    filler = w_in.shape[0] - inner
    w_in[pl.ds(inner, filler), :] = jnp.zeros((filler, width), BF16)
    w_out[pl.ds(inner, filler), :] = jnp.zeros((filler, width), BF16)

    @pl.loop(0, groups)
    def _(group):
        dispatch(group)

        @pl.when(group == 0)
        def _():
            pl.semaphore_wait(barrier, count - 1)

        @pl.when(group > 0)
        def _():
            have_left(sent.at[0], 0)

        to_all(sent.at[group], rows.at[group], group)

    weight_copies[0].wait()
    weight_copies[1].wait()

    @pl.loop(0, groups)
    def _(group):
        from_all(rows.at[group], group)
        experts(group)
        to_all(answers.at[group], returned.at[group], groups + group)

        @pl.when(group == 0)
        def _():
            line_texts[spot] = text_ref[...]
            texts[line] = text_ref[...]
            to_line(line_texts.at[spot], line_texts, 4)
            to_lines(texts, 5)

    text = text_ref[...]
    weight_copies[2].wait()
    weight_copies[3].wait()

    @pl.loop(0, groups)
    def _(group):
        from_all(returned.at[group], groups + group)
        pool(group)

    full = dot(headed[...], w_value[...])
    head_width = width // heads
    head = lax.rem(iota(full.shape, 0), heads)
    column = iota(full.shape, 1)
    own_head = (column >= head * head_width) & (column < (head + 1) * head_width)
    values = jnp.sum(jnp.where(own_head, full, 0.0).reshape(images, heads, width), axis=1)
    pooled = dot(values.astype(BF16), w_proj[...])
    result_ref[0] = pooled
    img_norm = norm_of(pooled)
    unit = pooled / img_norm
    line_units[spot] = unit.astype(BF16)
    units[line] = unit.astype(BF16)
    to_line(line_units.at[spot], line_units, 6)
    to_lines(units, 7)

    heat = jnp.exp(jnp.full((1, 1), heat_ref[0], F32))
    intercept = intercept_ref[0]
    pairs = images * count
    near, far = images * RING, images * lines
    row, col = iota((near, far), 0), iota((near, far), 1)
    own_row = (row >= spot * images) & (row < (spot + 1) * images)
    label = jnp.where(own_row & (row - spot * images == col - line * images), 1.0, -1.0)

    zeros = jnp.zeros((images, width), BF16)
    image_sums[spot] = zeros
    text_sums[spot] = zeros

    def own_block(part):
        return jnp.sum(jnp.where(own_row[:, 0:1], part, 0.0).reshape(RING, images, width), axis=0)

    def coefficients(cosines):
        scores = heat * cosines + intercept
        return -label * jax.nn.sigmoid(-label * scores) / pairs

    from_others(line_texts, 4)
    from_others(texts, 5)
    table = texts[...].reshape(far, width)
    table_norm = norm_of(table.astype(F32))
    table_norm = jnp.transpose(jnp.broadcast_to(table_norm, (far, 128)))[0:1, :]
    near_texts = line_texts[...].reshape(near, width)
    near_norms = norm_of(near_texts.astype(F32))
    text = text.astype(F32)
    text_norm = norm_of(text)
    unit_text = text / text_norm
    from_others(line_units, 6)
    cosines = dot(line_units[...].reshape(near, width), table, BY_ROWS) / table_norm
    part = heat * split_dot(coefficients(cosines) / table_norm, table)
    image_parts[...] = part.astype(BF16).reshape(RING, images, width)
    to_line(image_parts, image_sums, 8)
    own_image_part = own_block(part)

    from_others(units, 7)
    table = units[...].reshape(far, width)
    cosines = dot(near_texts, table, BY_ROWS) / near_norms
    part = heat * split_dot(coefficients(cosines), table)
    text_parts[...] = part.astype(BF16).reshape(RING, images, width)
    to_line(text_parts, text_sums, 9)
    own_text_part = own_block(part)

    from_others(image_sums, 8)
    grad = own_image_part + jnp.sum(image_sums[...].astype(F32), axis=0)
    result_ref[1] = (grad - unit * jnp.sum(unit * grad, axis=1, keepdims=True)) / img_norm
    from_others(text_sums, 9)
    grad = own_text_part + jnp.sum(text_sums[...].astype(F32), axis=0)
    result_ref[2] = (grad - unit_text * jnp.sum(unit_text * grad, axis=1, keepdims=True)) / text_norm

    blocks = [
        sent.at[1], answers.at[0], answers.at[1], line_texts, texts, line_units, units, image_parts, text_parts,
    ]
    for n, buffer in enumerate(blocks):
        have_left(buffer, n + 1)


def unstack(stacked_ref, pooled_ref, pooled_grad_ref, text_grad_ref, sem):
    copies = [
        pltpu.make_async_copy(stacked_ref.at[n], target, sem.at[n])
        for n, target in enumerate((pooled_ref, pooled_grad_ref, text_grad_ref))
    ]
    for copy in copies:
        copy.start()
    for copy in copies:
        copy.wait()


def body(
    patches, norm_gain, router, expert_in, expert_out, post_gain, key_query, value_proj, out_proj, text_embed,
    inverse_heat_exponent, score_intercept,
):
    images, patch_count, width = patches.shape
    inner = expert_out.shape[1]
    slots, heads = router.shape[1], key_query.shape[0]
    count = lax.axis_size("dp") * lax.axis_size("expert")
    groups = images // GROUP
    vmem = pl.BlockSpec(memory_space=pltpu.VMEM)
    hbm = pl.BlockSpec(memory_space=pl.ANY)
    filled = -(-inner // HIDDEN_STEP) * HIDDEN_STEP
    traffic = (groups, count, GROUP, width)
    out = jax.ShapeDtypeStruct((images, width), F32)
    result = pl.pallas_call(
        kernel,
        out_shape=jax.ShapeDtypeStruct((3, images, width), F32),
        in_specs=[hbm] * 10 + [pl.BlockSpec(memory_space=pltpu.SMEM)] * 2,
        out_specs=vmem,
        scratch_shapes=[
            pltpu.VMEM((width,), BF16),
            pltpu.VMEM(router.shape, BF16),
            pltpu.VMEM((width,), BF16),
            pltpu.VMEM(key_query.shape, BF16),
            pltpu.VMEM(text_embed.shape, BF16),
            pltpu.VMEM(patches.shape, BF16),
            pltpu.VMEM((filled, width), BF16),
            pltpu.VMEM((filled, width), BF16),
            pltpu.VMEM(value_proj.shape, BF16),
            pltpu.VMEM(out_proj.shape, BF16),
            pltpu.VMEM(traffic, BF16),
            pltpu.VMEM(traffic, BF16),
            pltpu.VMEM(traffic, BF16),
            pltpu.VMEM(traffic, BF16),
            pltpu.VMEM((count * GROUP, width), BF16),
            pltpu.VMEM((count * GROUP, filled), BF16),
            pltpu.VMEM((GROUP * patch_count, width), BF16),
            pltpu.VMEM((GROUP * patch_count, GROUP * slots), BF16),
            pltpu.VMEM((groups, GROUP * patch_count, GROUP * slots), BF16),
            pltpu.VMEM((images * heads, width), BF16),
            pltpu.VMEM((RING, images, width), BF16),
            pltpu.VMEM((count // RING, images, width), BF16),
            pltpu.VMEM((RING, images, width), BF16),
            pltpu.VMEM((count // RING, images, width), BF16),
            pltpu.VMEM((RING, images, width), BF16),
            pltpu.VMEM((RING, images, width), BF16),
            pltpu.VMEM((RING, images, width), BF16),
            pltpu.VMEM((RING, images, width), BF16),
            pltpu.SemaphoreType.DMA((images,)),
            pltpu.SemaphoreType.DMA((4,)),
            pltpu.SemaphoreType.DMA((5,)),
            pltpu.SemaphoreType.DMA((10,)),
            pltpu.SemaphoreType.DMA((10,)),
        ],
        compiler_params=pltpu.CompilerParams(
            collective_id=0, has_side_effects=True, vmem_limit_bytes=VMEM_BYTES
        ),
        cost_estimate=pl.CostEstimate(flops=12_000_000_000, bytes_accessed=40_000_000, transcendentals=4_000_000),
    )(
        patches, norm_gain, router, jnp.swapaxes(expert_in, 1, 2), expert_out, post_gain, key_query, value_proj,
        out_proj, text_embed, inverse_heat_exponent, score_intercept,
    )
    return pl.pallas_call(
        unstack,
        out_shape=(out, out, out),
        in_specs=[hbm],
        out_specs=(hbm, hbm, hbm),
        scratch_shapes=[pltpu.SemaphoreType.DMA((3,))],
        compiler_params=pltpu.CompilerParams(vmem_limit_bytes=VMEM_BYTES),
    )(result)


def solution(mesh):
    split = ("dp", "expert")
    placed = (
        P(split, None, None), P(), P(), P(split, None, None), P(split, None, None), P(), P(), P(), P(),
        P(split, None), P(), P(),
    )
    return jax.shard_map(
        body, mesh=mesh, in_specs=placed,
        out_specs=(P(split, None), P(split, None), P(split, None)), check_vma=False,
    )
```
